32 devices in a mesh: lon: 16 (over z, x, core), lat: 2 (over y).
Axes of the slice: x: 2, y: 2, z: 4, core: 2. Of those that a mesh axis runs over, the one named last changes fastest.
Arguments:
- adjoint_final: float32 [34, 256, 256], P(None, 'lon', 'lat'), may hold values from -6 to 6
- lon_courant: float32 [2, 34, 256, 256], P(None, None, 'lon', 'lat'), may hold values from -0.9 to 0.9
- lon_branch: int32 [2, 34, 256, 256], P(None, None, 'lon', 'lat'), may hold values from 0 to 2
- lat_courant: float32 [2, 34, 256, 256], P(None, None, 'lon', 'lat'), may hold values from -0.9 to 0.9
- lat_branch: int32 [2, 34, 256, 256], P(None, None, 'lon', 'lat'), may hold values from 0 to 2
- mixing: float32 [2, 33, 256, 256], P(None, None, 'lon', 'lat'), may hold values from 0.05 to 5
- region_map: int32 [256, 256], P('lon', 'lat'), may hold values from 0 to 8191
- region_order: int32 [8192], replicated, may hold values from 0 to 8191, each once
- prior_cov: float32 [32, 256, 256], P('lon'), may hold values from -0.4 to 0.4
Outputs:
- adjoint_start: float32 [34, 256, 256], P(None, 'lon', 'lat')
- flux_gradient: float32 [2, 8192], P(None, ('lon', 'lat'))
The draws below stay inside these ranges and needn't reach their ends.
Inputs may be any that keep to these rules, and one draw needn't show every extreme that they name: `region_order`: each position appears once.
All inputs are finite; a program needn't handle non-finite values.
Results may differ from the reference program's by a relative error of at most 0.0003.
Values sent between devices are 32-bit elements; how exact they have to be, the bound alone decides.
A program may use at most 128 MiB of HBM per device.

```python
import math
import jax
import jax.numpy as jnp
from jax import lax

LEV = 34
STEPS = 2
REGIONS = 8192
BLK = 256
NLON = 256
NLAT = 256
NBLK = 32


def draw_prior_cov(key, part):
    key_noise, key_scale = jax.random.split(jax.random.fold_in(key, 17))
    block_count = REGIONS // BLK
    noise = jnp.clip(jax.random.normal(key_noise, (block_count, BLK, BLK), jnp.float32), -6.0, 6.0)
    scales = jnp.exp(jax.random.uniform(key_scale, (block_count, BLK), jnp.float32, math.log(0.1), math.log(0.6)))
    mirrored = (noise + jnp.swapaxes(noise, 1, 2)) * (1.0 / math.sqrt(2.0))
    rows = lax.broadcasted_iota(jnp.int32, (BLK, BLK), 0)
    cols = lax.broadcasted_iota(jnp.int32, (BLK, BLK), 1)
    shaped = jnp.where(rows == cols, 1.0, mirrored * (0.3 / math.sqrt(BLK)))
    return shaped * scales[:, :, None] * scales[:, None, :]


def set_ends(values, own_key, least, top_value):
    index_at = [jax.random.randint(jax.random.fold_in(own_key, axis), (), 0, length) for axis, length in enumerate(values.shape)]
    main_axis = values.shape.index(max(values.shape))
    next_to = index_at[:main_axis] + [(index_at[main_axis] + 1) % values.shape[main_axis]] + index_at[main_axis + 1:]
    return values.at[tuple(index_at)].set(least).at[tuple(next_to)].set(top_value)


def level_of(key, extent, cuts, low, largest):
    factor_of, own = 1.0, jax.random.fold_in(key, 6)
    for axis_at, parts in cuts:
        heights = jnp.exp(jax.random.uniform(jax.random.fold_in(own, axis_at), (parts,), jnp.float32, low / len(cuts), largest / len(cuts)))
        factor_of = factor_of * jnp.repeat(heights, extent[axis_at] // parts).reshape([-1 if axis == axis_at else 1 for axis in range(len(extent))])
    return factor_of


def centred(rng, shape, deviation, bound, pieces=(), dtype=jnp.bfloat16):
    values = jax.random.normal(rng, shape, jnp.float32) * deviation
    if len(pieces) > 0:
        values = level_of(rng, shape, pieces, -0.22, 0.18) * values
    return jnp.clip(values, min=-bound, max=bound).astype(dtype)


def setup_inputs(seed: int = 0) -> dict:
    splits = jax.random.split(jax.random.key(seed), 10)
    adjoint_final = centred(splits[0], (LEV, NLON, NLAT), 1.0, 6.0, ((1, 16), (2, 2)), jnp.float32)
    lon_courant = jnp.clip(jax.random.uniform(splits[1], (STEPS, LEV, NLON, NLAT), jnp.float32, -0.9, 0.9) * level_of(splits[1], (STEPS, LEV, NLON, NLAT), ((2, 16), (3, 2)), -0.4, 0.0), -0.9, 0.9)
    lon_branch = set_ends(jax.random.randint(splits[2], (STEPS, LEV, NLON, NLAT), 0, 3), jax.random.fold_in(splits[2], 1), 0, 2).astype(jnp.int32)
    lat_courant = jnp.clip(jax.random.uniform(splits[3], (STEPS, LEV, NLON, NLAT), jnp.float32, -0.9, 0.9) * level_of(splits[3], (STEPS, LEV, NLON, NLAT), ((2, 16), (3, 2)), -0.4, 0.0), -0.9, 0.9)
    lat_branch = set_ends(jax.random.randint(splits[4], (STEPS, LEV, NLON, NLAT), 0, 3), jax.random.fold_in(splits[4], 1), 0, 2).astype(jnp.int32)
    mixing = jnp.clip(jnp.exp(math.log(5.0) - 4.6051702 * jax.random.uniform(splits[5], (STEPS, LEV - 1, NLON, NLAT), jnp.float32) ** level_of(splits[5], (STEPS, LEV - 1, NLON, NLAT), ((2, 16), (3, 2)), -0.2, 0.2)), 0.05, 5.0)
    region_map = set_ends(jax.random.randint(splits[6], (NLON, NLAT), 0, REGIONS), jax.random.fold_in(splits[6], 1), 0, REGIONS - 1).astype(jnp.int32)
    region_order = jax.random.permutation(splits[7], REGIONS).astype(jnp.int32)
    prior_cov = draw_prior_cov(jax.random.fold_in(splits[9], 71), 0)
    return dict(adjoint_final=adjoint_final, lon_courant=lon_courant, lon_branch=lon_branch, lat_courant=lat_courant, lat_branch=lat_branch, mixing=mixing, region_map=region_map, region_order=region_order, prior_cov=prior_cov)


def face_weights(courant, branch):
    half_step = 0.5 * (1.0 - jnp.abs(courant))
    lean_part = courant * half_step
    branch_one = jnp.where(branch == 1, 1.0, 0.0)
    branch_two = jnp.where(branch == 2, 1.0, 0.0)
    upwind_left = jnp.where(courant > 0.0, 1.0, 0.0)
    upwind_right = 1.0 - upwind_left
    donor = courant - branch_one * lean_part + branch_two * lean_part
    weight_far = -(upwind_left * branch_two * lean_part)
    weight_left = upwind_left * donor + upwind_right * branch_one * lean_part
    weight_right = upwind_left * branch_one * lean_part + upwind_right * donor
    weight_next = -(upwind_right * branch_two * lean_part)
    return [weight_far, weight_left, weight_right, weight_next]


def window(array, start, count, axis):
    return lax.slice_in_dim(array, start, start + count, axis=axis)


def transpose_flux(adjoint, padded, weights, axis):
    count = adjoint.shape[axis]
    jumps = window(padded, 1, count + 3, axis) - window(padded, 0, count + 3, axis)
    terms = [window(weight, 1, count + 3, axis) * jumps for weight in weights]
    result = adjoint + window(terms[0], 3, count, axis)
    result = result + window(terms[1], 2, count, axis)
    result = result + window(terms[2], 1, count, axis)
    return result + window(terms[3], 0, count, axis)


def vertical_solve(rhs, mixing):
    level_count = rhs.shape[0]
    ratios = []
    carried = []
    for level in range(level_count):
        if level == 0:
            denom = 1.0 + mixing[0]
            value = rhs[0] / denom
        else:
            lower = mixing[level - 1]
            diagonal = 1.0 + lower + mixing[level] if level < level_count - 1 else 1.0 + lower
            denom = diagonal + lower * ratios[-1]
            value = (rhs[level] + lower * carried[-1]) / denom
        ratios.append(-mixing[level] / denom if level < level_count - 1 else None)
        carried.append(value)
    result = [carried[-1]]
    for level in range(level_count - 2, -1, -1):
        result.insert(0, carried[level] - ratios[level] * result[0])
    return jnp.stack(result)


def horizontal(fields):
    adjoint, lon_c, lon_b, lat_c, lat_b = fields
    lat_weights = [jnp.pad(weight, ((0, 0), (2, 2))) for weight in face_weights(lat_c, lat_b)]
    adjoint = transpose_flux(adjoint, jnp.pad(adjoint, ((0, 0), (2, 2))), lat_weights, 1)
    lon_weights = [jnp.pad(weight, ((2, 2), (0, 0)), mode="wrap") for weight in face_weights(lon_c, lon_b)]
    return transpose_flux(adjoint, jnp.pad(adjoint, ((2, 2), (0, 0)), mode="wrap"), lon_weights, 0)


def reference(adjoint_final, lon_courant, lon_branch, lat_courant, lat_branch, mixing, region_map, region_order, prior_cov):
    lat_index = jnp.arange(NLAT)
    coslat = jnp.cos((lat_index.astype(jnp.float32) + 0.5) * (math.pi / NLAT) - 0.5 * math.pi)
    lat_inner = jnp.where(lat_index == 0, 0.0, lat_courant)
    adjoint = adjoint_final
    surface = [None] * STEPS
    for step in range(STEPS - 1, -1, -1):
        adjoint = vertical_solve(adjoint, mixing[step])
        adjoint = lax.map(horizontal, (adjoint, lon_courant[step], lon_branch[step], lat_inner[step], lat_branch[step]))
        surface[step] = adjoint[0] * coslat[None, :]
    field = jnp.stack(surface).reshape(STEPS, NLON * NLAT)
    slots = jnp.take(region_order, region_map.reshape(NLON * NLAT), axis=0)
    totals = jax.ops.segment_sum(field.T, slots, num_segments=REGIONS).T
    blocks = totals.reshape(STEPS, NBLK, BLK)
    mapped = jnp.einsum("sbj,bji->sbi", blocks, prior_cov, precision=lax.Precision.HIGHEST)
    return adjoint, mapped.reshape(STEPS, REGIONS)
```

```python
import functools
import math

import jax
import jax.numpy as jnp
import numpy as np
from jax import lax
from jax.experimental import pallas as pl
from jax.experimental.pallas import tpu as pltpu
from jax.sharding import PartitionSpec as P

MESH = pl.DeviceIdType.MESH
OWN = 8


def face_weights(courant, branch):
    lean_part = courant * (0.5 * (1.0 - jnp.abs(courant)))
    one_part = jnp.where(branch == 1, lean_part, 0.0)
    two_part = jnp.where(branch == 2, lean_part, 0.0)
    donor = courant - one_part + two_part
    left = courant > 0.0
    return (
        jnp.where(left, -two_part, 0.0),
        jnp.where(left, donor, one_part),
        jnp.where(left, one_part, donor),
        jnp.where(left, 0.0, -two_part),
    )


def kernel(
    nlon,
    nlat,
    width,
    adj_h,
    lonc_h,
    lonb_h,
    latc_h,
    latb_h,
    mix_h,
    cov_h,
    rmap_ref,
    order_ref,
    cos_ref,
    out_ref,
    flux_ref,
    x_ref,
    mixv,
    latc,
    latb,
    lonc,
    lonb,
    covv,
    inv_ref,
    kin_ref,
    nr_ref,
    y_ref,
    ext,
    lw,
    pack_w,
    land_w,
    pack_a,
    land_a,
    hi_ref,
    lo_ref,
    cht,
    amat,
    pscr,
    send_ref,
    land,
    local_sem,
    send_sem,
    recv_sem,
    all_sem,
):
    steps, levels, rows, lanes = latc.shape
    count = nlon * nlat
    my_lon, my_lat = lax.axis_index("lon"), lax.axis_index("lat")
    me = my_lon * nlat + my_lat
    blk = covv.shape[0]

    def place(device):
        return (device // nlat, lax.rem(device, nlat))

    barrier = pltpu.get_barrier_semaphore()

    def greet(k, carry):
        pl.semaphore_signal(
            barrier, inc=1, device_id=place(lax.rem(me + k, count)), device_id_type=MESH
        )
        return carry

    lax.fori_loop(1, count, greet, 0)

    def fetch(src, dst, slot):
        copy = pltpu.make_async_copy(src, dst, local_sem.at[slot])
        copy.start()
        return copy

    own = pl.ds(OWN, rows)
    get_mix = [None, None]
    get_mix[1] = fetch(mix_h.at[1], mixv.at[1], 0)
    get_adj = fetch(adj_h, x_ref, 1)
    get_latc = fetch(latc_h, latc, 2)
    get_latb = fetch(latb_h, latb, 3)
    get_lonc = fetch(lonc_h, lonc.at[:, :, own, :], 4)
    get_lonb = fetch(lonb_h, lonb.at[:, :, own, :], 5)
    get_mix[0] = fetch(mix_h.at[0], mixv.at[0], 6)
    get_cov = fetch(cov_h.at[(my_lat * width) // blk], covv, 7)

    lane = lax.broadcasted_iota(jnp.int32, (rows, lanes), 1)
    pair = lane // 2
    even = lax.rem(lane, 2) == 0
    zero = jnp.zeros((rows, lanes), jnp.float32)

    def roll(value, shift):
        return pltpu.roll(value, shift, 1)

    def remote(src, dst, slot, device):
        copy = pltpu.make_async_remote_copy(
            src_ref=src,
            dst_ref=dst,
            send_sem=send_sem.at[slot],
            recv_sem=recv_sem.at[slot],
            device_id=device,
            device_id_type=MESH,
        )
        copy.start()
        return copy

    north = (my_lon, lax.rem(my_lat + 1, nlat))
    south = (my_lon, lax.rem(my_lat + nlat - 1, nlat))
    east = (lax.rem(my_lon + 1, nlon), my_lat)
    west = (lax.rem(my_lon + nlon - 1, nlon), my_lat)

    def coefficients(s):
        k = mixv[s, 0]
        inv = 1.0 / (1.0 + k)
        inv_ref[s, 0] = inv
        kin_ref[s, 0] = zero
        nr_ref[s, 0] = k * inv

        def body(level, ahead):
            lower, k = mixv[s, level - 1], mixv[s, level]
            inv = 1.0 / ((1.0 + k) + lower * (1.0 - ahead))
            inv_ref[s, level] = inv
            kin_ref[s, level] = lower * inv
            ahead = k * inv
            nr_ref[s, level] = ahead
            return ahead

        ahead = lax.fori_loop(1, levels - 1, body, k * inv, unroll=True)
        lower = mixv[s, levels - 2]
        inv = 1.0 / (1.0 + lower * (1.0 - ahead))
        inv_ref[s, levels - 1] = inv
        kin_ref[s, levels - 1] = lower * inv
        nr_ref[s, levels - 1] = zero

    def tail_head(value, level, tail, head):
        turned = roll(value, 2 * level + 2)
        return jnp.where(pair == level, turned, tail), jnp.where(pair == level + 1, turned, head)

    def solve(s):
        def up(level, carried):
            carried = x_ref[level] * inv_ref[s, level] + kin_ref[s, level] * carried
            y_ref[level] = carried
            return carried

        lax.fori_loop(0, levels, up, zero, unroll=True)

        def down(i, carry):
            value, tail, head = carry
            level = levels - 1 - i
            value = y_ref[level] + nr_ref[s, level] * value
            y_ref[level] = value
            return (value,) + tail_head(value, level, tail, head)

        _, tail, head = lax.fori_loop(0, levels, down, (zero, zero, zero), unroll=True)
        pack_a[s, 0] = tail
        pack_a[s, 1] = roll(head, lanes - 2)

    def pack_weights(s):
        def body(level, carry):
            ct, ch, bt, bh = carry
            ct, ch = tail_head(latc[s, level], level, ct, ch)
            bt, bh = tail_head(latb[s, level].astype(jnp.float32), level, bt, bh)
            return ct, ch, bt, bh

        ct, ch, bt, bh = lax.fori_loop(0, levels, body, (zero,) * 4, unroll=True)
        pack_w[0, s, 0] = ct
        pack_w[0, s, 1] = bt
        pack_w[1, s, 0] = roll(ch, lanes - 2)
        pack_w[1, s, 1] = roll(bh, lanes - 2)

    def lat_inner(s):
        def body(level, carry):
            a = y_ref[level]
            m2, m1, m0, p1 = face_weights(latc[s, level], latb[s, level])
            jump = jnp.where(lane >= 1, a - roll(a, 1), 0.0)
            out = a + m0 * jump + roll(m1 * jump, lanes - 1)
            out = out + roll(jnp.where(lane >= 2, m2 * jump, 0.0), lanes - 2)
            out = out + roll(jnp.where(lane <= lanes - 2, p1 * jump, 0.0), 1)
            ext[s, level, OWN : OWN + rows] = out
            return carry

        lax.fori_loop(0, levels, body, 0, unroll=True)

    def lat_edges(s):
        tail, head = pack_a[s, 0], pack_a[s, 1]
        before, after = land_a[s, 0], land_a[s, 1]
        m2_after, m1_after, _, _ = face_weights(land_w[1, s, 0], land_w[1, s, 1])
        _, _, m0_head, p1_head = face_weights(pack_w[1, s, 0], pack_w[1, s, 1])
        _, _, _, p1_before = face_weights(land_w[0, s, 0], land_w[0, s, 1])
        jump = after - jnp.where(even, roll(tail, lanes - 1), roll(after, 1))
        top = m2_after * jump + roll(jnp.where(even, m1_after * jump, 0.0), 1)
        top = jnp.where(my_lat < nlat - 1, top, 0.0)
        jump = jnp.where(even, head - roll(before, lanes - 1), before - roll(before, 1))
        flux = jnp.where(even, p1_head, p1_before) * jump
        low = jnp.where(even, m0_head * jump + roll(flux, lanes - 1), roll(flux, 1))
        low = roll(jnp.where(my_lat > 0, low, 0.0), 2)
        first = lax.rem(lane, 4) < 2
        both = (jnp.where(first, top, low), jnp.where(first, low, top))
        edge = jnp.logical_or(lane < 2, lane >= lanes - 2)

        def body(m, carry):
            for odd in range(2):
                level = 2 * m + odd
                turned = roll(both[odd], lanes - 2 - 2 * level)
                ext[s, level, OWN : OWN + rows] += jnp.where(edge, turned, 0.0)
            return carry

        lax.fori_loop(0, levels // 2, body, 0, unroll=True)

    def lon_own_weights(s):
        def body(level, carry):
            found = face_weights(
                lonc[s, level, OWN : OWN + rows], lonb[s, level, OWN : OWN + rows]
            )
            for member in range(4):
                lw[s, member, level, OWN : OWN + rows] = found[member]
            return carry

        lax.fori_loop(0, levels, body, 0, unroll=True)

    def lon_far_weights(s):
        def body(level, carry):
            found = face_weights(lonc[s, level, OWN - 2 : OWN], lonb[s, level, OWN - 2 : OWN])
            lw[s, 3, level, OWN - 2 : OWN] = found[3]
            end = OWN + rows
            found = face_weights(lonc[s, level, end : end + 2], lonb[s, level, end : end + 2])
            lw[s, 0, level, end : end + 2] = found[0]
            lw[s, 1, level, end : end + 2] = found[1]
            return carry

        lax.fori_loop(0, levels, body, 0, unroll=True)

    def lon_level(s, level):
        a = [ext[s, level, OWN + k : OWN + k + rows] for k in range(-2, 3)]
        w = [
            lw[s, member, level, OWN + 2 - member : OWN + 2 - member + rows]
            for member in range(4)
        ]
        out = a[2] + w[0] * (a[4] - a[3]) + w[1] * (a[3] - a[2])
        return out + w[2] * (a[2] - a[1]) + w[3] * (a[1] - a[0])

    def send_rows(buffer_at, at_dst, base):
        last = pl.ds(OWN + rows - 2, 2)
        return (
            remote(buffer_at(last), at_dst(pl.ds(OWN - 2, 2)), base, east),
            remote(buffer_at(pl.ds(OWN, 2)), at_dst(pl.ds(OWN + rows, 2)), base + 1, west),
        )

    def find_slots():
        order = order_ref[...]
        table = jnp.concatenate([order // 128, lax.rem(order, 128)], axis=0)
        table = table.astype(jnp.float32).astype(jnp.bfloat16)
        high = order.shape[0]
        down = lax.broadcasted_iota(jnp.int32, (lanes, lanes), 0)
        row_of = lax.broadcasted_iota(jnp.int32, (high, lanes), 0)
        for i in range(rows):
            region = rmap_ref[i : i + 1, :]
            hit = jnp.where(down == lax.rem(region, 128), 1.0, 0.0).astype(jnp.bfloat16)
            found = jnp.dot(table, hit, preferred_element_type=jnp.float32)
            here = row_of == region // 128
            hi = jnp.sum(jnp.where(here, found[:high], 0.0), axis=0, keepdims=True)
            lo = jnp.sum(jnp.where(here, found[high:], 0.0), axis=0, keepdims=True)
            hi_ref[i : i + 1, :] = hi
            cht[:, i * lanes : (i + 1) * lanes] = jnp.where(
                down.astype(jnp.float32) == lo, 1.0, 0.0
            ).astype(jnp.bfloat16)

    def regions(s, field):
        high = order_ref.shape[0]
        row_of = lax.broadcasted_iota(jnp.int32, (high, lanes), 0).astype(jnp.float32)
        lo_ref[...] = field
        for i in range(rows):
            here = row_of == hi_ref[i : i + 1, :]
            spread = jnp.where(here, lo_ref[i : i + 1, :], 0.0)
            coarse = spread.astype(jnp.bfloat16)
            fine = (spread - coarse.astype(jnp.float32)).astype(jnp.bfloat16)
            amat[:high, i * lanes : (i + 1) * lanes] = coarse
            amat[high:, i * lanes : (i + 1) * lanes] = fine
        sums = lax.dot_general(
            amat[...], cht[...], (((1,), (1,)), ((), ())), preferred_element_type=jnp.float32
        )
        pscr[...] = sums[:high] + sums[high:]
        for group in range(high // 2):
            send_ref[group, 2 * s : 2 * s + 2, :] = pscr[2 * group : 2 * group + 2, :]

    get_mix[1].wait()
    coefficients(1)
    get_latc.wait()
    get_latb.wait()
    for s in range(steps):
        pack_weights(s)
    get_adj.wait()
    solve(1)
    pl.semaphore_wait(barrier, count - 1)

    arriving = []
    lat_a = {}
    lat_a[1] = (
        remote(pack_a.at[1, 0], land_a.at[1, 0], 0, north),
        remote(pack_a.at[1, 1], land_a.at[1, 1], 1, south),
    )
    lat_w = (
        remote(pack_w.at[0], land_w.at[0], 2, north),
        remote(pack_w.at[1], land_w.at[1], 3, south),
    )
    get_lonc.wait()
    get_lonb.wait()
    lon_c = send_rows(
        lambda at: lonc.at[:, :, at, :], lambda at: lonc.at[:, :, at, :], 4
    )
    lon_b = send_rows(
        lambda at: lonb.at[:, :, at, :], lambda at: lonb.at[:, :, at, :], 6
    )
    lat_inner(1)
    lon_own_weights(1)
    for copy in lat_a[1] + lat_w:
        copy.wait_recv()
    lat_edges(1)
    lon_a = {}
    lon_a[1] = send_rows(
        lambda at: ext.at[1, :, at, :], lambda at: ext.at[1, :, at, :], 8
    )
    get_mix[0].wait()
    coefficients(0)
    find_slots()
    lon_own_weights(0)
    for copy in lon_c + lon_b:
        copy.wait_recv()
    for s in (1, 0):
        lon_far_weights(s)
    for copy in lon_a[1]:
        copy.wait_recv()

    def middle(level, carry):
        x_ref[level] = lon_level(1, level)
        return carry

    lax.fori_loop(0, levels, middle, 0, unroll=True)
    cosine = cos_ref[pl.ds(my_lat, 1), 0, :]
    solve(0)
    lat_a[0] = (
        remote(pack_a.at[0, 0], land_a.at[0, 0], 10, north),
        remote(pack_a.at[0, 1], land_a.at[0, 1], 11, south),
    )
    lat_inner(0)
    for copy in lat_a[0]:
        copy.wait_recv()
    lat_edges(0)
    lon_a[0] = send_rows(
        lambda at: ext.at[0, :, at, :], lambda at: ext.at[0, :, at, :], 12
    )
    regions(1, x_ref[0] * cosine)
    for copy in lon_a[0]:
        copy.wait_recv()
    start = lon_level(0, 0)
    out_ref[0] = start
    regions(0, start * cosine)

    def group_of(device):
        return (device * width) // blk

    def scatter(k, carry):
        device = lax.rem(me + k, count)
        pltpu.make_async_remote_copy(
            src_ref=send_ref.at[group_of(device)],
            dst_ref=land.at[me],
            send_sem=all_sem.at[0],
            recv_sem=all_sem.at[1],
            device_id=place(device),
            device_id_type=MESH,
        ).start()
        return carry

    lax.fori_loop(1, count, scatter, 0)
    land[me] = send_ref[group_of(me)]

    def last(level, carry):
        out_ref[level] = lon_level(0, level)
        return carry

    lax.fori_loop(1, levels, last, 0, unroll=True)
    get_cov.wait()
    for copy in lat_a[1] + lat_w + lon_c + lon_b + lon_a[1] + lat_a[0] + lon_a[0]:
        copy.wait_send()
    every = land.at[pl.ds(0, count - 1)]
    pltpu.make_async_copy(every, every, all_sem.at[0]).wait()
    pltpu.make_async_copy(every, every, all_sem.at[1]).wait()
    totals = jnp.sum(land[...], axis=0)
    half = blk // 2
    one = jnp.dot(
        totals, covv[:half], precision=lax.Precision.HIGHEST, preferred_element_type=jnp.float32
    )
    two = jnp.dot(
        totals, covv[half:], precision=lax.Precision.HIGHEST, preferred_element_type=jnp.float32
    )
    for s in range(steps):
        flux_ref[s : s + 1, :] = one[2 * s : 2 * s + 1] + two[2 * s + 1 : 2 * s + 2]


def per_device(
    nlon,
    nlat,
    adjoint_final,
    lon_courant,
    lon_branch,
    lat_courant,
    lat_branch,
    mixing,
    region_map,
    region_order,
    prior_cov,
):
    steps, levels, rows, lanes = lon_courant.shape
    regions = region_order.shape[0]
    blk = prior_cov.shape[1]
    width = regions // (nlon * nlat)
    lat_total = lanes * nlat
    lat_index = np.arange(lat_total, dtype=np.float32)
    angle = (lat_index + np.float32(0.5)) * np.float32(math.pi / lat_total)
    cosines = np.cos((angle - np.float32(0.5 * math.pi)).astype(np.float32))
    cosines = jnp.asarray(cosines.astype(np.float32).reshape(nlat, 1, lanes))
    f32, i32, b16 = jnp.float32, jnp.int32, jnp.bfloat16
    field = (levels, rows, lanes)
    tall = (levels, rows + 2 * OWN, lanes)
    vm = pltpu.VMEM
    scratch = [
        vm(field, f32),
        vm((steps, levels - 1, rows, lanes), f32),
        vm((steps,) + field, f32),
        vm((steps,) + field, i32),
        vm((steps,) + tall, f32),
        vm((steps,) + tall, i32),
        vm((blk, blk), f32),
        vm((steps,) + field, f32),
        vm((steps,) + field, f32),
        vm((steps,) + field, f32),
        vm(field, f32),
        vm((steps,) + tall, f32),
        vm((steps, 4) + tall, f32),
        vm((2, steps, 2, rows, lanes), f32),
        vm((2, steps, 2, rows, lanes), f32),
        vm((steps, 2, rows, lanes), f32),
        vm((steps, 2, rows, lanes), f32),
        vm((rows, lanes), f32),
        vm((rows, lanes), f32),
        vm((128, rows * lanes), b16),
        vm((2 * (regions // 128), rows * lanes), b16),
        vm((regions // 128, 128), f32),
        vm((regions // blk, 4, 128), f32),
        vm((nlon * nlat, 4, 128), f32),
        pltpu.SemaphoreType.DMA((8,)),
        pltpu.SemaphoreType.DMA((14,)),
        pltpu.SemaphoreType.DMA((14,)),
        pltpu.SemaphoreType.DMA((2,)),
    ]
    adjoint, flux = pl.pallas_call(
        functools.partial(kernel, nlon, nlat, width),
        out_shape=(
            jax.ShapeDtypeStruct(field, f32),
            jax.ShapeDtypeStruct((steps, blk), f32),
        ),
        in_specs=[pl.BlockSpec(memory_space=pl.ANY)] * 7
        + [pl.BlockSpec(memory_space=pltpu.VMEM)] * 3,
        out_specs=(
            pl.BlockSpec(memory_space=pltpu.VMEM),
            pl.BlockSpec(memory_space=pltpu.VMEM),
        ),
        scratch_shapes=scratch,
        compiler_params=pltpu.CompilerParams(
            collective_id=0, has_side_effects=True, vmem_limit_bytes=40 * 1024 * 1024
        ),
    )(
        adjoint_final,
        lon_courant,
        lon_branch,
        lat_courant,
        lat_branch,
        mixing,
        prior_cov,
        region_map,
        region_order.reshape(regions // 128, 128),
        cosines,
    )
    if width < blk:
        start = lax.rem(lax.axis_index("lat") * width, blk)
        flux = lax.dynamic_slice_in_dim(flux, start, width, 1)
    return adjoint, flux


def solution(mesh):
    four = P(None, None, "lon", "lat")
    placed = (
        P(None, "lon", "lat"),
        four,
        four,
        four,
        four,
        four,
        P("lon", "lat"),
        P(),
        P("lon", None, None),
    )
    return jax.shard_map(
        functools.partial(per_device, mesh.shape["lon"], mesh.shape["lat"]),
        mesh=mesh,
        in_specs=placed,
        out_specs=(P(None, "lon", "lat"), P(None, ("lon", "lat"))),
        check_vma=False,
    )
```

```python
import functools
import math

import jax
import jax.numpy as jnp
import numpy as np
from jax import lax
from jax.experimental import pallas as pl
from jax.experimental.pallas import tpu as pltpu
from jax.sharding import PartitionSpec as P

MESH = pl.DeviceIdType.MESH
OWN = 8


def face_weights(courant, branch):
    lean_part = courant * (0.5 * (1.0 - jnp.abs(courant)))
    one_part = jnp.where(branch == 1, lean_part, 0.0)
    two_part = jnp.where(branch == 2, lean_part, 0.0)
    donor = courant - one_part + two_part
    left = courant > 0.0
    return (
        jnp.where(left, -two_part, 0.0),
        jnp.where(left, donor, one_part),
        jnp.where(left, one_part, donor),
        jnp.where(left, 0.0, -two_part),
    )


def kernel(
    nlon,
    nlat,
    width,
    adj_h,
    lonc_h,
    lonb_h,
    latc_h,
    latb_h,
    mix_h,
    cov_h,
    rmap_h,
    order_h,
    cos_h,
    out_ref,
    flux_ref,
    rmap_ref,
    order_ref,
    cos_ref,
    x_ref,
    mixv,
    latc,
    latb,
    lonc,
    lonb,
    covv,
    inv_ref,
    kin_ref,
    nr_ref,
    y_ref,
    ext,
    lw,
    pack_w,
    land_w,
    pack_a,
    land_a,
    rows_a,
    far_a,
    rows_w,
    far_w,
    far_out,
    hi_ref,
    lo_ref,
    cht,
    amat,
    pscr,
    send_ref,
    land,
    local_sem,
    send_sem,
    recv_sem,
    all_sem,
):
    steps, levels, rows, lanes = latc.shape
    count = nlon * nlat
    my_lon, my_lat = lax.axis_index("lon"), lax.axis_index("lat")
    me = my_lon * nlat + my_lat
    blk = covv.shape[0]

    def place(device):
        return (device // nlat, lax.rem(device, nlat))

    barrier = pltpu.get_barrier_semaphore()

    def greet(k, carry):
        pl.semaphore_signal(
            barrier, inc=1, device_id=place(lax.rem(me + k, count)), device_id_type=MESH
        )
        return carry

    lax.fori_loop(1, count, greet, 0)

    def fetch(src, dst, slot):
        copy = pltpu.make_async_copy(src, dst, local_sem.at[slot])
        copy.start()
        return copy

    own = pl.ds(OWN, rows)
    get_mix = [None, None]
    get_mix[1] = fetch(mix_h.at[1], mixv.at[1], 0)
    get_adj = fetch(adj_h, x_ref, 1)
    get_latc = fetch(latc_h, latc, 2)
    get_latb = fetch(latb_h, latb, 3)
    get_lonc = fetch(lonc_h, lonc.at[:, :, own, :], 4)
    get_lonb = fetch(lonb_h, lonb.at[:, :, own, :], 5)
    get_mix[0] = fetch(mix_h.at[0], mixv.at[0], 6)
    get_cov = fetch(cov_h.at[(my_lat * width) // blk], covv, 7)
    get_small = (
        fetch(rmap_h, rmap_ref, 8),
        fetch(order_h, order_ref, 9),
        fetch(cos_h.at[my_lat], cos_ref, 10),
    )

    lane = lax.broadcasted_iota(jnp.int32, (rows, lanes), 1)
    pair = lane // 2
    even = lax.rem(lane, 2) == 0
    zero = jnp.zeros((rows, lanes), jnp.float32)

    def roll(value, shift):
        return pltpu.roll(value, shift, 1)

    def remote(src, dst, slot, device):
        copy = pltpu.make_async_remote_copy(
            src_ref=src,
            dst_ref=dst,
            send_sem=send_sem.at[slot],
            recv_sem=recv_sem.at[slot],
            device_id=device,
            device_id_type=MESH,
        )
        copy.start()
        return copy

    north = (my_lon, lax.rem(my_lat + 1, nlat))
    south = (my_lon, lax.rem(my_lat + nlat - 1, nlat))
    east = (lax.rem(my_lon + 1, nlon), my_lat)
    west = (lax.rem(my_lon + nlon - 1, nlon), my_lat)

    def coefficients(s):
        k = mixv[s, 0]
        inv = 1.0 / (1.0 + k)
        inv_ref[s, 0] = inv
        kin_ref[s, 0] = zero
        nr_ref[s, 0] = k * inv

        def body(level, ahead):
            lower, k = mixv[s, level - 1], mixv[s, level]
            inv = 1.0 / ((1.0 + k) + lower * (1.0 - ahead))
            inv_ref[s, level] = inv
            kin_ref[s, level] = lower * inv
            ahead = k * inv
            nr_ref[s, level] = ahead
            return ahead

        ahead = lax.fori_loop(1, levels - 1, body, k * inv, unroll=True)
        lower = mixv[s, levels - 2]
        inv = 1.0 / (1.0 + lower * (1.0 - ahead))
        inv_ref[s, levels - 1] = inv
        kin_ref[s, levels - 1] = lower * inv
        nr_ref[s, levels - 1] = zero

    def tail_head(value, level, tail, head):
        turned = roll(value, 2 * level + 2)
        return jnp.where(pair == level, turned, tail), jnp.where(pair == level + 1, turned, head)

    def solve(s):
        def up(level, carried):
            carried = x_ref[level] * inv_ref[s, level] + kin_ref[s, level] * carried
            y_ref[level] = carried
            return carried

        lax.fori_loop(0, levels, up, zero, unroll=True)

        def down(i, carry):
            value, tail, head = carry
            level = levels - 1 - i
            value = y_ref[level] + nr_ref[s, level] * value
            y_ref[level] = value
            rows_a[0, s, pl.ds(2 * level, 2), :] = value[rows - 2 :]
            rows_a[1, s, pl.ds(2 * level, 2), :] = value[:2]
            return (value,) + tail_head(value, level, tail, head)

        _, tail, head = lax.fori_loop(0, levels, down, (zero, zero, zero), unroll=True)
        head = roll(head, lanes - 2)
        for member, value in enumerate((tail, head)):
            pack_a[s, member, OWN : OWN + rows] = value
            at = 2 * levels + 2 * member
            rows_a[0, s, at : at + 2] = value[rows - 2 :]
            rows_a[1, s, at : at + 2] = value[:2]

    def pack_weights(s):
        def body(level, carry):
            ct, ch, bt, bh = carry
            ct, ch = tail_head(latc[s, level], level, ct, ch)
            both = (latc[s, level], latb[s, level].astype(jnp.float32))
            bt, bh = tail_head(both[1], level, bt, bh)
            for member in range(2):
                rows_w[0, s, member, pl.ds(2 * level, 2), :] = both[member][rows - 2 :]
                rows_w[1, s, member, pl.ds(2 * level, 2), :] = both[member][:2]
            return ct, ch, bt, bh

        ct, ch, bt, bh = lax.fori_loop(0, levels, body, (zero,) * 4, unroll=True)
        found = ((ct, bt), (roll(ch, lanes - 2), roll(bh, lanes - 2)))
        for end in range(2):
            at = 2 * levels + 2 * end
            for member in range(2):
                value = found[end][member]
                pack_w[end, s, member, OWN : OWN + rows] = value
                rows_w[0, s, member, at : at + 2] = value[rows - 2 :]
                rows_w[1, s, member, at : at + 2] = value[:2]

    def lat_pass(a, courant, branch):
        at = lax.broadcasted_iota(jnp.int32, a.shape, 1)
        m2, m1, m0, p1 = face_weights(courant, branch)
        jump = jnp.where(at >= 1, a - roll(a, 1), 0.0)
        out = a + m0 * jump + roll(m1 * jump, lanes - 1)
        out = out + roll(jnp.where(at >= 2, m2 * jump, 0.0), lanes - 2)
        return out + roll(jnp.where(at <= lanes - 2, p1 * jump, 0.0), 1)

    def lat_inner(s):
        def body(level, carry):
            out = lat_pass(y_ref[level], latc[s, level], latb[s, level])
            ext[s, level, OWN : OWN + rows] = out
            return carry

        lax.fori_loop(0, levels, body, 0, unroll=True)

    def lat_edges(s):
        at = 2 * levels
        lane = lax.broadcasted_iota(jnp.int32, (rows + 2 * OWN, lanes), 1)
        even = lax.rem(lane, 2) == 0
        for side, where in enumerate((slice(OWN - 2, OWN), slice(OWN + rows, OWN + rows + 2))):
            far_out[side] = lat_pass(far_a[side, s], far_w[side, s, 0], far_w[side, s, 1])
            for member in range(2):
                pack_a[s, member, where] = far_a[side, s, at + 2 * member : at + 2 * member + 2]
                pack_w[1, s, member, where] = far_w[side, s, member, at + 2 : at + 4]
        tail, head = pack_a[s, 0], pack_a[s, 1]
        before, after = land_a[s, 0], land_a[s, 1]
        m2_after, m1_after, _, _ = face_weights(land_w[1, s, 0], land_w[1, s, 1])
        _, _, m0_head, p1_head = face_weights(pack_w[1, s, 0], pack_w[1, s, 1])
        _, _, _, p1_before = face_weights(land_w[0, s, 0], land_w[0, s, 1])
        jump = after - jnp.where(even, roll(tail, lanes - 1), roll(after, 1))
        top = m2_after * jump + roll(jnp.where(even, m1_after * jump, 0.0), 1)
        top = jnp.where(my_lat < nlat - 1, top, 0.0)
        jump = jnp.where(even, head - roll(before, lanes - 1), before - roll(before, 1))
        flux = jnp.where(even, p1_head, p1_before) * jump
        low = jnp.where(even, m0_head * jump + roll(flux, lanes - 1), roll(flux, 1))
        low = roll(jnp.where(my_lat > 0, low, 0.0), 2)
        first = lax.rem(lane, 4) < 2
        both = (jnp.where(first, top, low), jnp.where(first, low, top))
        edge = jnp.logical_or(lane < 2, lane >= lanes - 2)

        def body(m, carry):
            for odd in range(2):
                level = 2 * m + odd
                turned = jnp.where(edge, roll(both[odd], lanes - 2 - 2 * level), 0.0)
                ext[s, level, OWN : OWN + rows] += turned[OWN : OWN + rows]
                two = pl.ds(2 * level, 2)
                end = OWN + rows
                ext[s, level, OWN - 2 : OWN] = far_out[0, two, :] + turned[OWN - 2 : OWN]
                ext[s, level, end : end + 2] = far_out[1, two, :] + turned[end : end + 2]
            return carry

        lax.fori_loop(0, levels // 2, body, 0, unroll=True)

    def lon_own_weights(s):
        def body(level, carry):
            found = face_weights(
                lonc[s, level, OWN : OWN + rows], lonb[s, level, OWN : OWN + rows]
            )
            for member in range(4):
                lw[s, member, level, OWN : OWN + rows] = found[member]
            return carry

        lax.fori_loop(0, levels, body, 0, unroll=True)

    def lon_far_weights(s):
        def body(level, carry):
            found = face_weights(lonc[s, level, OWN - 2 : OWN], lonb[s, level, OWN - 2 : OWN])
            lw[s, 3, level, OWN - 2 : OWN] = found[3]
            end = OWN + rows
            found = face_weights(lonc[s, level, end : end + 2], lonb[s, level, end : end + 2])
            lw[s, 0, level, end : end + 2] = found[0]
            lw[s, 1, level, end : end + 2] = found[1]
            return carry

        lax.fori_loop(0, levels, body, 0, unroll=True)

    def lon_level(s, level):
        a = [ext[s, level, OWN + k : OWN + k + rows] for k in range(-2, 3)]
        w = [
            lw[s, member, level, OWN + 2 - member : OWN + 2 - member + rows]
            for member in range(4)
        ]
        out = a[2] + w[0] * (a[4] - a[3]) + w[1] * (a[3] - a[2])
        return out + w[2] * (a[2] - a[1]) + w[3] * (a[1] - a[0])

    def send_rows(buffer_at, at_dst, base):
        last = pl.ds(OWN + rows - 2, 2)
        return (
            remote(buffer_at(last), at_dst(pl.ds(OWN - 2, 2)), base, east),
            remote(buffer_at(pl.ds(OWN, 2)), at_dst(pl.ds(OWN + rows, 2)), base + 1, west),
        )

    def find_slots():
        order = order_ref[...]
        table = jnp.concatenate([order // 128, lax.rem(order, 128)], axis=0)
        table = table.astype(jnp.float32).astype(jnp.bfloat16)
        high = order.shape[0]
        down = lax.broadcasted_iota(jnp.int32, (lanes, lanes), 0)
        row_of = lax.broadcasted_iota(jnp.int32, (high, lanes), 0)
        for i in range(rows):
            region = rmap_ref[i : i + 1, :]
            hit = jnp.where(down == lax.rem(region, 128), 1.0, 0.0).astype(jnp.bfloat16)
            found = jnp.dot(table, hit, preferred_element_type=jnp.float32)
            here = row_of == region // 128
            hi = jnp.sum(jnp.where(here, found[:high], 0.0), axis=0, keepdims=True)
            lo = jnp.sum(jnp.where(here, found[high:], 0.0), axis=0, keepdims=True)
            hi_ref[i : i + 1, :] = hi
            cht[:, i * lanes : (i + 1) * lanes] = jnp.where(
                down.astype(jnp.float32) == lo, 1.0, 0.0
            ).astype(jnp.bfloat16)

    def regions(s, field):
        high = order_ref.shape[0]
        row_of = lax.broadcasted_iota(jnp.int32, (high, lanes), 0).astype(jnp.float32)
        lo_ref[...] = field
        for i in range(rows):
            here = row_of == hi_ref[i : i + 1, :]
            spread = jnp.where(here, lo_ref[i : i + 1, :], 0.0)
            coarse = spread.astype(jnp.bfloat16)
            fine = (spread - coarse.astype(jnp.float32)).astype(jnp.bfloat16)
            amat[:high, i * lanes : (i + 1) * lanes] = coarse
            amat[high:, i * lanes : (i + 1) * lanes] = fine
        sums = lax.dot_general(
            amat[...], cht[...], (((1,), (1,)), ((), ())), preferred_element_type=jnp.float32
        )
        pscr[...] = sums[:high] + sums[high:]
        for group in range(high // 2):
            send_ref[group, 2 * s : 2 * s + 2, :] = pscr[2 * group : 2 * group + 2, :]

    get_mix[1].wait()
    coefficients(1)
    get_latc.wait()
    get_latb.wait()
    for s in range(steps):
        pack_weights(s)
    get_adj.wait()
    solve(1)
    pl.semaphore_wait(barrier, count - 1)

    turn = {1: lax.rem(my_lon + 1, nlon), -1: lax.rem(my_lon + nlon - 1, nlon)}
    own_rows, first, last_two = pl.ds(OWN, rows), pl.ds(OWN, 2), pl.ds(OWN + rows - 2, 2)
    low, high = pl.ds(OWN - 2, 2), pl.ds(OWN + rows, 2)

    def send_columns(source, target, base):
        copies = []
        for end in range(2):
            beside = (north, south)[end][1]
            for k, (lon, src, dst) in enumerate(
                (
                    (my_lon, own_rows, own_rows),
                    (turn[1], last_two, low),
                    (turn[-1], first, high),
                )
            ):
                copies.append(
                    remote(source(end, src), target(end, dst), base + 3 * end + k, (lon, beside))
                )
        return tuple(copies)

    def exchange(s, base):
        return (
            remote(rows_a.at[0, s], far_a.at[0, s], base, east),
            remote(rows_a.at[1, s], far_a.at[1, s], base + 1, west),
        ) + send_columns(
            lambda end, at: pack_a.at[s, end, at, :],
            lambda end, at: land_a.at[s, end, at, :],
            base + 2,
        )

    def send_far_weights(s, base):
        return (
            remote(rows_w.at[0, s], far_w.at[0, s], base, east),
            remote(rows_w.at[1, s], far_w.at[1, s], base + 1, west),
        )

    sent_a = {1: exchange(1, 0)}
    sent_w = {1: send_far_weights(1, 8)}
    lat_w = send_columns(
        lambda end, at: pack_w.at[end, :, :, at, :],
        lambda end, at: land_w.at[end, :, :, at, :],
        10,
    )
    get_lonc.wait()
    get_lonb.wait()
    lon_c = send_rows(lambda at: lonc.at[:, :, at, :], lambda at: lonc.at[:, :, at, :], 16)
    lon_b = send_rows(lambda at: lonb.at[:, :, at, :], lambda at: lonb.at[:, :, at, :], 18)
    sent_w[0] = send_far_weights(0, 20)
    lat_inner(1)
    lon_own_weights(1)
    get_mix[0].wait()
    coefficients(0)
    for copy in sent_a[1] + sent_w[1] + lat_w:
        copy.wait_recv()
    lat_edges(1)
    for copy in lon_c + lon_b:
        copy.wait_recv()
    lon_far_weights(1)

    def middle(level, carry):
        x_ref[level] = lon_level(1, level)
        return carry

    lax.fori_loop(0, levels, middle, 0, unroll=True)
    solve(0)
    sent_a[0] = exchange(0, 22)
    lat_inner(0)
    lon_own_weights(0)
    lon_far_weights(0)
    for copy in get_small:
        copy.wait()
    cosine = cos_ref[...]
    find_slots()
    regions(1, x_ref[0] * cosine)
    for copy in sent_a[0] + sent_w[0]:
        copy.wait_recv()
    lat_edges(0)
    start = lon_level(0, 0)
    out_ref[0] = start
    regions(0, start * cosine)

    def group_of(device):
        return (device * width) // blk

    def scatter(k, carry):
        device = lax.rem(me + k, count)
        pltpu.make_async_remote_copy(
            src_ref=send_ref.at[group_of(device)],
            dst_ref=land.at[me],
            send_sem=all_sem.at[0],
            recv_sem=all_sem.at[1],
            device_id=place(device),
            device_id_type=MESH,
        ).start()
        return carry

    lax.fori_loop(1, count, scatter, 0)
    land[me] = send_ref[group_of(me)]

    def last(level, carry):
        out_ref[level] = lon_level(0, level)
        return carry

    lax.fori_loop(1, levels, last, 0, unroll=True)
    get_cov.wait()
    for copy in sent_a[1] + sent_a[0] + sent_w[1] + sent_w[0] + lat_w + lon_c + lon_b:
        copy.wait_send()
    every = land.at[pl.ds(0, count - 1)]
    pltpu.make_async_copy(every, every, all_sem.at[0]).wait()
    pltpu.make_async_copy(every, every, all_sem.at[1]).wait()
    totals = jnp.sum(land[...], axis=0)
    half = blk // 2
    one = jnp.dot(
        totals, covv[:half], precision=lax.Precision.HIGHEST, preferred_element_type=jnp.float32
    )
    two = jnp.dot(
        totals, covv[half:], precision=lax.Precision.HIGHEST, preferred_element_type=jnp.float32
    )
    for s in range(steps):
        flux_ref[s : s + 1, :] = one[2 * s : 2 * s + 1] + two[2 * s + 1 : 2 * s + 2]


def per_device(
    nlon,
    nlat,
    adjoint_final,
    lon_courant,
    lon_branch,
    lat_courant,
    lat_branch,
    mixing,
    region_map,
    region_order,
    prior_cov,
):
    steps, levels, rows, lanes = lon_courant.shape
    regions = region_order.shape[0]
    blk = prior_cov.shape[1]
    width = regions // (nlon * nlat)
    lat_total = lanes * nlat
    lat_index = np.arange(lat_total, dtype=np.float32)
    angle = (lat_index + np.float32(0.5)) * np.float32(math.pi / lat_total)
    cosines = np.cos((angle - np.float32(0.5 * math.pi)).astype(np.float32))
    cosines = jnp.asarray(cosines.astype(np.float32).reshape(nlat, 1, lanes))
    f32, i32, b16 = jnp.float32, jnp.int32, jnp.bfloat16
    field = (levels, rows, lanes)
    tall = (levels, rows + 2 * OWN, lanes)
    vm = pltpu.VMEM
    scratch = [
        vm((rows, lanes), i32),
        vm((regions // 128, 128), i32),
        vm((1, lanes), f32),
        vm(field, f32),
        vm((steps, levels - 1, rows, lanes), f32),
        vm((steps,) + field, f32),
        vm((steps,) + field, i32),
        vm((steps,) + tall, f32),
        vm((steps,) + tall, i32),
        vm((blk, blk), f32),
        vm((steps,) + field, f32),
        vm((steps,) + field, f32),
        vm((steps,) + field, f32),
        vm(field, f32),
        vm((steps,) + tall, f32),
        vm((steps, 4) + tall, f32),
        vm((2, steps, 2, rows + 2 * OWN, lanes), f32),
        vm((2, steps, 2, rows + 2 * OWN, lanes), f32),
        vm((steps, 2, rows + 2 * OWN, lanes), f32),
        vm((steps, 2, rows + 2 * OWN, lanes), f32),
        vm((2, steps, 2 * levels + 4, lanes), f32),
        vm((2, steps, 2 * levels + 4, lanes), f32),
        vm((2, steps, 2, 2 * levels + 4, lanes), f32),
        vm((2, steps, 2, 2 * levels + 4, lanes), f32),
        vm((2, 2 * levels + 4, lanes), f32),
        vm((rows, lanes), f32),
        vm((rows, lanes), f32),
        vm((128, rows * lanes), b16),
        vm((2 * (regions // 128), rows * lanes), b16),
        vm((regions // 128, 128), f32),
        vm((regions // blk, 4, 128), f32),
        vm((nlon * nlat, 4, 128), f32),
        pltpu.SemaphoreType.DMA((11,)),
        pltpu.SemaphoreType.DMA((30,)),
        pltpu.SemaphoreType.DMA((30,)),
        pltpu.SemaphoreType.DMA((2,)),
    ]
    adjoint, flux = pl.pallas_call(
        functools.partial(kernel, nlon, nlat, width),
        out_shape=(
            jax.ShapeDtypeStruct(field, f32),
            jax.ShapeDtypeStruct((steps, blk), f32),
        ),
        in_specs=[pl.BlockSpec(memory_space=pltpu.HBM)] * 10,
        out_specs=(
            pl.BlockSpec(memory_space=pltpu.VMEM),
            pl.BlockSpec(memory_space=pltpu.VMEM),
        ),
        scratch_shapes=scratch,
        compiler_params=pltpu.CompilerParams(
            collective_id=0, has_side_effects=True, vmem_limit_bytes=61 * 1024 * 1024
        ),
    )(
        adjoint_final,
        lon_courant,
        lon_branch,
        lat_courant,
        lat_branch,
        mixing,
        prior_cov,
        region_map,
        region_order.reshape(regions // 128, 128),
        cosines,
    )
    if width < blk:
        start = lax.rem(lax.axis_index("lat") * width, blk)
        flux = lax.dynamic_slice_in_dim(flux, start, width, 1)
    return adjoint, flux


def solution(mesh):
    four = P(None, None, "lon", "lat")
    placed = (
        P(None, "lon", "lat"),
        four,
        four,
        four,
        four,
        four,
        P("lon", "lat"),
        P(),
        P("lon", None, None),
    )
    return jax.shard_map(
        functools.partial(per_device, mesh.shape["lon"], mesh.shape["lat"]),
        mesh=mesh,
        in_specs=placed,
        out_specs=(P(None, "lon", "lat"), P(None, ("lon", "lat"))),
        check_vma=False,
    )
```

```python
import functools
import math

import jax
import jax.numpy as jnp
import numpy as np
from jax import lax
from jax.experimental import pallas as pl
from jax.experimental.pallas import tpu as pltpu
from jax.sharding import PartitionSpec as P

MESH = pl.DeviceIdType.MESH
OWN = 8


def face_weights(courant, branch):
    lean_part = courant * (0.5 * (1.0 - jnp.abs(courant)))
    one_part = jnp.where(branch == 1, lean_part, 0.0)
    two_part = jnp.where(branch == 2, lean_part, 0.0)
    donor = courant - one_part + two_part
    left = courant > 0.0
    return (
        jnp.where(left, -two_part, 0.0),
        jnp.where(left, donor, one_part),
        jnp.where(left, one_part, donor),
        jnp.where(left, 0.0, -two_part),
    )


def kernel(
    nlon,
    nlat,
    width,
    adj_h,
    lonc_h,
    lonb_h,
    latc_h,
    latb_h,
    mix_h,
    cov_h,
    rmap_h,
    order_h,
    cos_h,
    out_ref,
    flux_ref,
    rmap_ref,
    order_ref,
    cos_ref,
    x_ref,
    mixv,
    latc,
    latb,
    lonc,
    lonb,
    covv,
    inv_ref,
    kin_ref,
    nr_ref,
    y_ref,
    ext,
    lw,
    pack_w,
    land_w,
    pack_a,
    land_a,
    rows_a,
    far_a,
    rows_w,
    far_w,
    far_out,
    hi_ref,
    lo_ref,
    cht,
    amat,
    pscr,
    send_ref,
    land,
    local_sem,
    send_sem,
    recv_sem,
    all_sem,
):
    steps, levels, rows, lanes = latc.shape
    count = nlon * nlat
    my_lon, my_lat = lax.axis_index("lon"), lax.axis_index("lat")
    me = my_lon * nlat + my_lat
    blk = covv.shape[0]

    def place(device):
        return (device // nlat, lax.rem(device, nlat))

    barrier = pltpu.get_barrier_semaphore()

    def greet(k, carry):
        pl.semaphore_signal(
            barrier, inc=1, device_id=place(lax.rem(me + k, count)), device_id_type=MESH
        )
        return carry

    lax.fori_loop(1, count, greet, 0)

    def fetch(src, dst, slot):
        copy = pltpu.make_async_copy(src, dst, local_sem.at[slot])
        copy.start()
        return copy

    own = pl.ds(OWN, rows)
    get_mix = [None, None]
    get_mix[1] = fetch(mix_h.at[1], mixv.at[1], 0)
    get_adj = fetch(adj_h, x_ref, 1)
    get_latc = fetch(latc_h, latc, 2)
    get_latb = fetch(latb_h, latb, 3)
    get_lonc = fetch(lonc_h, lonc.at[:, :, own, :], 4)
    get_lonb = fetch(lonb_h, lonb.at[:, :, own, :], 5)
    get_mix[0] = fetch(mix_h.at[0], mixv.at[0], 6)
    get_cov = fetch(cov_h.at[(my_lat * width) // blk], covv, 7)
    get_small = (
        fetch(rmap_h, rmap_ref, 8),
        fetch(order_h, order_ref, 9),
        fetch(cos_h.at[my_lat], cos_ref, 10),
    )

    lane = lax.broadcasted_iota(jnp.int32, (rows, lanes), 1)
    pair = lane // 2
    even = lax.rem(lane, 2) == 0
    zero = jnp.zeros((rows, lanes), jnp.float32)

    def roll(value, shift):
        return pltpu.roll(value, shift, 1)

    def remote(src, dst, slot, device):
        copy = pltpu.make_async_remote_copy(
            src_ref=src,
            dst_ref=dst,
            send_sem=send_sem.at[slot],
            recv_sem=recv_sem.at[slot],
            device_id=device,
            device_id_type=MESH,
        )
        copy.start()
        return copy

    north = (my_lon, lax.rem(my_lat + 1, nlat))
    south = (my_lon, lax.rem(my_lat + nlat - 1, nlat))
    east = (lax.rem(my_lon + 1, nlon), my_lat)
    west = (lax.rem(my_lon + nlon - 1, nlon), my_lat)

    def coefficients(s):
        k = mixv[s, 0]
        inv = 1.0 / (1.0 + k)
        inv_ref[s, 0] = inv
        kin_ref[s, 0] = zero
        nr_ref[s, 0] = k * inv

        def body(level, ahead):
            lower, k = mixv[s, level - 1], mixv[s, level]
            inv = 1.0 / ((1.0 + k) + lower * (1.0 - ahead))
            inv_ref[s, level] = inv
            kin_ref[s, level] = lower * inv
            ahead = k * inv
            nr_ref[s, level] = ahead
            return ahead

        ahead = lax.fori_loop(1, levels - 1, body, k * inv, unroll=True)
        lower = mixv[s, levels - 2]
        inv = 1.0 / (1.0 + lower * (1.0 - ahead))
        inv_ref[s, levels - 1] = inv
        kin_ref[s, levels - 1] = lower * inv
        nr_ref[s, levels - 1] = zero

    def tail_head(value, level, tail, head):
        turned = roll(value, 2 * level + 2)
        return jnp.where(pair == level, turned, tail), jnp.where(pair == level + 1, turned, head)

    def solve(s):
        def up(level, carried):
            carried = x_ref[level] * inv_ref[s, level] + kin_ref[s, level] * carried
            y_ref[level] = carried
            return carried

        lax.fori_loop(0, levels, up, zero, unroll=True)

        def down(i, carry):
            value, tail, head = carry
            level = levels - 1 - i
            value = y_ref[level] + nr_ref[s, level] * value
            y_ref[level] = value
            rows_a[0, s, pl.ds(2 * level, 2), :] = value[rows - 2 :]
            rows_a[1, s, pl.ds(2 * level, 2), :] = value[:2]
            return (value,) + tail_head(value, level, tail, head)

        _, tail, head = lax.fori_loop(0, levels, down, (zero, zero, zero), unroll=True)
        head = roll(head, lanes - 2)
        for member, value in enumerate((tail, head)):
            pack_a[s, member, OWN : OWN + rows] = value
            at = 2 * levels + 2 * member
            rows_a[0, s, at : at + 2] = value[rows - 2 :]
            rows_a[1, s, at : at + 2] = value[:2]

    def pack_weights(s):
        def body(level, carry):
            ct, ch, bt, bh = carry
            ct, ch = tail_head(latc[s, level], level, ct, ch)
            both = (latc[s, level], latb[s, level].astype(jnp.float32))
            bt, bh = tail_head(both[1], level, bt, bh)
            for member in range(2):
                rows_w[0, s, member, pl.ds(2 * level, 2), :] = both[member][rows - 2 :]
                rows_w[1, s, member, pl.ds(2 * level, 2), :] = both[member][:2]
            return ct, ch, bt, bh

        ct, ch, bt, bh = lax.fori_loop(0, levels, body, (zero,) * 4, unroll=True)
        found = ((ct, bt), (roll(ch, lanes - 2), roll(bh, lanes - 2)))
        for end in range(2):
            at = 2 * levels + 2 * end
            for member in range(2):
                value = found[end][member]
                pack_w[end, s, member, OWN : OWN + rows] = value
                rows_w[0, s, member, at : at + 2] = value[rows - 2 :]
                rows_w[1, s, member, at : at + 2] = value[:2]

    def lat_pass(a, courant, branch):
        at = lax.broadcasted_iota(jnp.int32, a.shape, 1)
        m2, m1, m0, p1 = face_weights(courant, branch)
        jump = jnp.where(at >= 1, a - roll(a, 1), 0.0)
        out = a + m0 * jump + roll(m1 * jump, lanes - 1)
        out = out + roll(jnp.where(at >= 2, m2 * jump, 0.0), lanes - 2)
        return out + roll(jnp.where(at <= lanes - 2, p1 * jump, 0.0), 1)

    def lat_inner(s):
        def body(level, carry):
            out = lat_pass(y_ref[level], latc[s, level], latb[s, level])
            ext[s, level, OWN : OWN + rows] = out
            return carry

        lax.fori_loop(0, levels, body, 0, unroll=True)

    def lat_edges(s):
        at = 2 * levels
        lane = lax.broadcasted_iota(jnp.int32, (rows + 2 * OWN, lanes), 1)
        even = lax.rem(lane, 2) == 0
        for side, where in enumerate((slice(OWN - 2, OWN), slice(OWN + rows, OWN + rows + 2))):
            far_out[side] = lat_pass(far_a[side, s], far_w[side, s, 0], far_w[side, s, 1])
            for member in range(2):
                pack_a[s, member, where] = far_a[side, s, at + 2 * member : at + 2 * member + 2]
                pack_w[1, s, member, where] = far_w[side, s, member, at + 2 : at + 4]
        tail, head = pack_a[s, 0], pack_a[s, 1]
        before, after = land_a[s, 0], land_a[s, 1]
        m2_after, m1_after, _, _ = face_weights(land_w[1, s, 0], land_w[1, s, 1])
        _, _, m0_head, p1_head = face_weights(pack_w[1, s, 0], pack_w[1, s, 1])
        _, _, _, p1_before = face_weights(land_w[0, s, 0], land_w[0, s, 1])
        jump = after - jnp.where(even, roll(tail, lanes - 1), roll(after, 1))
        top = m2_after * jump + roll(jnp.where(even, m1_after * jump, 0.0), 1)
        top = jnp.where(my_lat < nlat - 1, top, 0.0)
        jump = jnp.where(even, head - roll(before, lanes - 1), before - roll(before, 1))
        flux = jnp.where(even, p1_head, p1_before) * jump
        low = jnp.where(even, m0_head * jump + roll(flux, lanes - 1), roll(flux, 1))
        low = roll(jnp.where(my_lat > 0, low, 0.0), 2)
        first = lax.rem(lane, 4) < 2
        both = (jnp.where(first, top, low), jnp.where(first, low, top))
        edge = jnp.logical_or(lane < 2, lane >= lanes - 2)

        def body(m, carry):
            for odd in range(2):
                level = 2 * m + odd
                turned = jnp.where(edge, roll(both[odd], lanes - 2 - 2 * level), 0.0)
                ext[s, level, OWN : OWN + rows] += turned[OWN : OWN + rows]
                two = pl.ds(2 * level, 2)
                end = OWN + rows
                ext[s, level, OWN - 2 : OWN] = far_out[0, two, :] + turned[OWN - 2 : OWN]
                ext[s, level, end : end + 2] = far_out[1, two, :] + turned[end : end + 2]
            return carry

        lax.fori_loop(0, levels // 2, body, 0, unroll=True)

    def lon_own_weights(s):
        def body(level, carry):
            found = face_weights(
                lonc[s, level, OWN : OWN + rows], lonb[s, level, OWN : OWN + rows]
            )
            for member in range(4):
                lw[s, member, level, OWN : OWN + rows] = found[member]
            return carry

        lax.fori_loop(0, levels, body, 0, unroll=True)

    def lon_far_weights(s):
        def body(level, carry):
            found = face_weights(lonc[s, level, OWN - 2 : OWN], lonb[s, level, OWN - 2 : OWN])
            lw[s, 3, level, OWN - 2 : OWN] = found[3]
            end = OWN + rows
            found = face_weights(lonc[s, level, end : end + 2], lonb[s, level, end : end + 2])
            lw[s, 0, level, end : end + 2] = found[0]
            lw[s, 1, level, end : end + 2] = found[1]
            return carry

        lax.fori_loop(0, levels, body, 0, unroll=True)

    def lon_level(s, level):
        a = [ext[s, level, OWN + k : OWN + k + rows] for k in range(-2, 3)]
        w = [
            lw[s, member, level, OWN + 2 - member : OWN + 2 - member + rows]
            for member in range(4)
        ]
        out = a[2] + w[0] * (a[4] - a[3]) + w[1] * (a[3] - a[2])
        return out + w[2] * (a[2] - a[1]) + w[3] * (a[1] - a[0])

    def send_rows(buffer_at, at_dst, base):
        last = pl.ds(OWN + rows - 2, 2)
        return (
            remote(buffer_at(last), at_dst(pl.ds(OWN - 2, 2)), base, east),
            remote(buffer_at(pl.ds(OWN, 2)), at_dst(pl.ds(OWN + rows, 2)), base + 1, west),
        )

    def find_slots():
        order = order_ref[...]
        table = jnp.concatenate([order // 128, lax.rem(order, 128)], axis=0)
        table = table.astype(jnp.float32).astype(jnp.bfloat16)
        high = order.shape[0]
        down = lax.broadcasted_iota(jnp.int32, (lanes, lanes), 0)
        row_of = lax.broadcasted_iota(jnp.int32, (high, lanes), 0)
        for i in range(rows):
            region = rmap_ref[i : i + 1, :]
            hit = jnp.where(down == lax.rem(region, 128), 1.0, 0.0).astype(jnp.bfloat16)
            found = jnp.dot(table, hit, preferred_element_type=jnp.float32)
            here = row_of == region // 128
            hi = jnp.sum(jnp.where(here, found[:high], 0.0), axis=0, keepdims=True)
            lo = jnp.sum(jnp.where(here, found[high:], 0.0), axis=0, keepdims=True)
            hi_ref[i : i + 1, :] = hi
            cht[:, i * lanes : (i + 1) * lanes] = jnp.where(
                down.astype(jnp.float32) == lo, 1.0, 0.0
            ).astype(jnp.bfloat16)

    def regions(s, field):
        high = order_ref.shape[0]
        row_of = lax.broadcasted_iota(jnp.int32, (high, lanes), 0).astype(jnp.float32)
        lo_ref[...] = field
        for i in range(rows):
            here = row_of == hi_ref[i : i + 1, :]
            spread = jnp.where(here, lo_ref[i : i + 1, :], 0.0)
            coarse = spread.astype(jnp.bfloat16)
            fine = (spread - coarse.astype(jnp.float32)).astype(jnp.bfloat16)
            amat[:high, i * lanes : (i + 1) * lanes] = coarse
            amat[high:, i * lanes : (i + 1) * lanes] = fine
        sums = lax.dot_general(
            amat[...], cht[...], (((1,), (1,)), ((), ())), preferred_element_type=jnp.float32
        )
        pscr[...] = sums[:high] + sums[high:]
        for group in range(high // 2):
            send_ref[group, 2 * s : 2 * s + 2, :] = pscr[2 * group : 2 * group + 2, :]

    get_mix[1].wait()
    coefficients(1)
    get_latc.wait()
    get_latb.wait()
    for s in range(steps):
        pack_weights(s)
    get_adj.wait()
    solve(1)
    pl.semaphore_wait(barrier, count - 1)

    turn = {1: lax.rem(my_lon + 1, nlon), -1: lax.rem(my_lon + nlon - 1, nlon)}
    own_rows, first, last_two = pl.ds(OWN, rows), pl.ds(OWN, 2), pl.ds(OWN + rows - 2, 2)
    low, high = pl.ds(OWN - 2, 2), pl.ds(OWN + rows, 2)

    def send_columns(source, target, base):
        copies = []
        for end in range(2):
            beside = (north, south)[end][1]
            for k, (lon, src, dst) in enumerate(
                (
                    (my_lon, own_rows, own_rows),
                    (turn[1], last_two, low),
                    (turn[-1], first, high),
                )
            ):
                copies.append(
                    remote(source(end, src), target(end, dst), base + 3 * end + k, (lon, beside))
                )
        return tuple(copies)

    def exchange(s, base):
        return (
            remote(rows_a.at[0, s], far_a.at[0, s], base, east),
            remote(rows_a.at[1, s], far_a.at[1, s], base + 1, west),
        ) + send_columns(
            lambda end, at: pack_a.at[s, end, at, :],
            lambda end, at: land_a.at[s, end, at, :],
            base + 2,
        )

    def send_far_weights(s, base):
        return (
            remote(rows_w.at[0, s], far_w.at[0, s], base, east),
            remote(rows_w.at[1, s], far_w.at[1, s], base + 1, west),
        )

    sent_a = {1: exchange(1, 0)}
    sent_w = {1: send_far_weights(1, 8)}
    lat_w = send_columns(
        lambda end, at: pack_w.at[end, :, :, at, :],
        lambda end, at: land_w.at[end, :, :, at, :],
        10,
    )
    get_lonc.wait()
    get_lonb.wait()

    def send_lon(s, base):
        return send_rows(
            lambda at: lonc.at[s, :, at, :], lambda at: lonc.at[s, :, at, :], base
        ) + send_rows(lambda at: lonb.at[s, :, at, :], lambda at: lonb.at[s, :, at, :], base + 2)

    sent_lon = {1: send_lon(1, 16)}
    lat_inner(1)
    lon_own_weights(1)
    get_mix[0].wait()
    coefficients(0)
    for copy in sent_a[1] + sent_w[1] + lat_w:
        copy.wait_recv()
    sent_w[0] = send_far_weights(0, 20)
    sent_lon[0] = send_lon(0, 30)
    lat_edges(1)
    for copy in sent_lon[1]:
        copy.wait_recv()
    lon_far_weights(1)

    def middle(level, carry):
        x_ref[level] = lon_level(1, level)
        return carry

    lax.fori_loop(0, levels, middle, 0, unroll=True)
    solve(0)
    sent_a[0] = exchange(0, 22)
    lat_inner(0)
    lon_own_weights(0)
    for copy in get_small:
        copy.wait()
    cosine = cos_ref[...]
    find_slots()
    regions(1, x_ref[0] * cosine)
    for copy in sent_lon[0]:
        copy.wait_recv()
    lon_far_weights(0)
    for copy in sent_a[0] + sent_w[0]:
        copy.wait_recv()
    lat_edges(0)
    start = lon_level(0, 0)
    out_ref[0] = start
    regions(0, start * cosine)

    def group_of(device):
        return (device * width) // blk

    def scatter(k, carry):
        device = lax.rem(me + k, count)
        pltpu.make_async_remote_copy(
            src_ref=send_ref.at[group_of(device)],
            dst_ref=land.at[me],
            send_sem=all_sem.at[0],
            recv_sem=all_sem.at[1],
            device_id=place(device),
            device_id_type=MESH,
        ).start()
        return carry

    lax.fori_loop(1, count, scatter, 0)
    land[me] = send_ref[group_of(me)]

    def last(level, carry):
        out_ref[level] = lon_level(0, level)
        return carry

    lax.fori_loop(1, levels, last, 0, unroll=True)
    get_cov.wait()
    for copy in sent_a[1] + sent_a[0] + sent_w[1] + sent_w[0] + lat_w + sent_lon[1] + sent_lon[0]:
        copy.wait_send()
    every = land.at[pl.ds(0, count - 1)]
    pltpu.make_async_copy(every, every, all_sem.at[0]).wait()
    pltpu.make_async_copy(every, every, all_sem.at[1]).wait()
    totals = jnp.sum(land[...], axis=0)
    half = blk // 2
    one = jnp.dot(
        totals, covv[:half], precision=lax.Precision.HIGHEST, preferred_element_type=jnp.float32
    )
    two = jnp.dot(
        totals, covv[half:], precision=lax.Precision.HIGHEST, preferred_element_type=jnp.float32
    )
    for s in range(steps):
        flux_ref[s : s + 1, :] = one[2 * s : 2 * s + 1] + two[2 * s + 1 : 2 * s + 2]


def per_device(
    nlon,
    nlat,
    adjoint_final,
    lon_courant,
    lon_branch,
    lat_courant,
    lat_branch,
    mixing,
    region_map,
    region_order,
    prior_cov,
):
    steps, levels, rows, lanes = lon_courant.shape
    regions = region_order.shape[0]
    blk = prior_cov.shape[1]
    width = regions // (nlon * nlat)
    lat_total = lanes * nlat
    lat_index = np.arange(lat_total, dtype=np.float32)
    angle = (lat_index + np.float32(0.5)) * np.float32(math.pi / lat_total)
    cosines = np.cos((angle - np.float32(0.5 * math.pi)).astype(np.float32))
    cosines = jnp.asarray(cosines.astype(np.float32).reshape(nlat, 1, lanes))
    f32, i32, b16 = jnp.float32, jnp.int32, jnp.bfloat16
    field = (levels, rows, lanes)
    tall = (levels, rows + 2 * OWN, lanes)
    vm = pltpu.VMEM
    scratch = [
        vm((rows, lanes), i32),
        vm((regions // 128, 128), i32),
        vm((1, lanes), f32),
        vm(field, f32),
        vm((steps, levels - 1, rows, lanes), f32),
        vm((steps,) + field, f32),
        vm((steps,) + field, i32),
        vm((steps,) + tall, f32),
        vm((steps,) + tall, i32),
        vm((blk, blk), f32),
        vm((steps,) + field, f32),
        vm((steps,) + field, f32),
        vm((steps,) + field, f32),
        vm(field, f32),
        vm((steps,) + tall, f32),
        vm((steps, 4) + tall, f32),
        vm((2, steps, 2, rows + 2 * OWN, lanes), f32),
        vm((2, steps, 2, rows + 2 * OWN, lanes), f32),
        vm((steps, 2, rows + 2 * OWN, lanes), f32),
        vm((steps, 2, rows + 2 * OWN, lanes), f32),
        vm((2, steps, 2 * levels + 4, lanes), f32),
        vm((2, steps, 2 * levels + 4, lanes), f32),
        vm((2, steps, 2, 2 * levels + 4, lanes), f32),
        vm((2, steps, 2, 2 * levels + 4, lanes), f32),
        vm((2, 2 * levels + 4, lanes), f32),
        vm((rows, lanes), f32),
        vm((rows, lanes), f32),
        vm((128, rows * lanes), b16),
        vm((2 * (regions // 128), rows * lanes), b16),
        vm((regions // 128, 128), f32),
        vm((regions // blk, 4, 128), f32),
        vm((nlon * nlat, 4, 128), f32),
        pltpu.SemaphoreType.DMA((11,)),
        pltpu.SemaphoreType.DMA((34,)),
        pltpu.SemaphoreType.DMA((34,)),
        pltpu.SemaphoreType.DMA((2,)),
    ]
    adjoint, flux = pl.pallas_call(
        functools.partial(kernel, nlon, nlat, width),
        out_shape=(
            pltpu.VMEM(field, f32),
            pltpu.VMEM((steps, blk), f32),
        ),
        in_specs=[pl.BlockSpec(memory_space=pltpu.HBM)] * 10,
        out_specs=(
            pl.BlockSpec(memory_space=pltpu.VMEM),
            pl.BlockSpec(memory_space=pltpu.VMEM),
        ),
        scratch_shapes=scratch,
        compiler_params=pltpu.CompilerParams(
            collective_id=0, has_side_effects=True, vmem_limit_bytes=61 * 1024 * 1024
        ),
    )(
        adjoint_final,
        lon_courant,
        lon_branch,
        lat_courant,
        lat_branch,
        mixing,
        prior_cov,
        region_map,
        region_order.reshape(regions // 128, 128),
        cosines,
    )
    if width < blk:
        start = lax.rem(lax.axis_index("lat") * width, blk)
        flux = lax.dynamic_slice_in_dim(flux, start, width, 1)
    return adjoint, flux


def solution(mesh):
    four = P(None, None, "lon", "lat")
    placed = (
        P(None, "lon", "lat"),
        four,
        four,
        four,
        four,
        four,
        P("lon", "lat"),
        P(),
        P("lon", None, None),
    )
    return jax.shard_map(
        functools.partial(per_device, mesh.shape["lon"], mesh.shape["lat"]),
        mesh=mesh,
        in_specs=placed,
        out_specs=(P(None, "lon", "lat"), P(None, ("lon", "lat"))),
        check_vma=False,
    )
```
